32 devices in a mesh: elem: 8 (over y, x, core), mode: 4 (over z).
Axes of the slice: x: 2, y: 2, z: 4, core: 2. Of those that a mesh axis runs over, the one named last changes fastest.
Arguments:
- iterate: float32 [480, 8192], P('mode', 'elem'), may hold values from -0.75 to 0.75
- newton_residual: float32 [480, 8192], P('mode', 'elem'), may hold values from -6 to 6
- inverse_blocks: float32 [64, 8192], P(None, 'elem'), may hold values from -0.15 to 2
- basis_values: bfloat16 [1024, 480], replicated, may hold values from -4 to 4, as said below
- triple_blocks: bfloat16 [8, 60, 20160], P('mode', None, 'elem'), may hold values from -0.375 to 0.375
- block_columns: int32 [8, 4], P('mode'), may hold values from 0 to 7, as said below
- neighbour_ids: int32 [128, 6], P('elem'), may hold values from 0 to 15, as said below
Outputs:
- correction: float32 [480, 8192], P('mode', 'elem')
- linear_residual: float32 [480, 8192], P('mode', 'elem')
The draws below stay inside these ranges and needn't reach their ends.
Inputs may be any that keep to these rules, and one draw needn't show every extreme that they name: `neighbour_ids`: columns 0 to 3 give the neighbour across the -y, +y, -z, +z faces within the element's own block of 16 elements; columns 4 and 5 the neighbour across the -x and +x faces within the previous and the next block, cyclically. Neighbours are mutual across opposite faces. `block_columns`: row b names 4 different block columns; the first is b. `basis_values`: column 0 holds ones, the constant mode.
All inputs are finite; a program needn't handle non-finite values.
Results may differ from the reference program's by a relative error of at most 0.0039.
Values may be sent and summed in bfloat16 or wider, within the bound.
A program may use at most 128 MiB of HBM per device.

```python
import math
import jax
import jax.numpy as jnp
import numpy as np
from jax import lax

P_SIZE = 480
K = 84
S = 1024
Q = 64
NB = 8
NNZB = 4
ITERS = 2
E_DEV = 16
MB = 60
NODES = 8192
N_ELEM = 8


def draw_basis_values(key, part):
    subkey = jax.random.fold_in(key, 11)
    values = jax.random.truncated_normal(subkey, -4.0, 4.0, (S, P_SIZE), jnp.float32)
    constant_column = jnp.arange(P_SIZE) == 0
    return jnp.where(constant_column[None, :], 1.0, values).astype(jnp.bfloat16)


def draw_inverse_blocks(key, part):
    node_total = E_DEV * Q * N_ELEM
    diagonal_key = jax.random.fold_in(key, 21)
    spread_key = jax.random.fold_in(key, 22)
    diagonal = jax.random.uniform(diagonal_key, (1, node_total), jnp.float32, 0.5, 1.5)
    spread = jax.random.truncated_normal(spread_key, -4.0, 4.0, (Q, node_total), jnp.float32) * (0.3 / math.sqrt(Q))
    source_rows = jnp.arange(Q)[:, None]
    target_rows = (jnp.arange(node_total) % Q)[None, :]
    return jnp.where(source_rows == target_rows, diagonal, spread).astype(jnp.float32)


def draw_block_columns(key, part):
    keys_list = jax.random.split(jax.random.fold_in(key, 5), NB)

    def one_row(subkey, row_index):
        others = jax.random.permutation(subkey, NB - 1) + 1
        return (row_index + others[:NNZB - 1]) % NB
    rest = jax.vmap(one_row)(keys_list, jnp.arange(NB))
    return jnp.concatenate([jnp.arange(NB)[:, None], rest], axis=1).astype(jnp.int32)


def draw_neighbour_ids(key, part):
    rows_across = E_DEV // 2
    keys_list = jax.random.split(jax.random.fold_in(key, 7), N_ELEM)
    orders = jax.vmap(lambda subkey: jax.random.permutation(subkey, E_DEV))(keys_list)
    places = jnp.argsort(orders, axis=1)
    blocks = jnp.arange(N_ELEM)[:, None]
    along_y = places // 2
    along_z = places % 2

    def lookup(block_index, y_index, z_index):
        return orders[block_index % N_ELEM, y_index % rows_across * 2 + z_index % 2]
    columns = [lookup(blocks, along_y - 1, along_z), lookup(blocks, along_y + 1, along_z), lookup(blocks, along_y, along_z - 1), lookup(blocks, along_y, along_z + 1), lookup(blocks - 1, along_y, along_z), lookup(blocks + 1, along_y, along_z)]
    return jnp.stack(columns, axis=-1).reshape(N_ELEM * E_DEV, 6).astype(jnp.int32)


def shard_levels(rng, dims, cuts, low, largest):
    factor_of = 1.0
    for position, parts in cuts:
        steps = jax.random.uniform(jax.random.fold_in(jax.random.fold_in(rng, 6), position), (parts,), jnp.float32, low / len(cuts), largest / len(cuts))
        factor_of = factor_of * jnp.repeat(jnp.exp(steps), dims[position] // parts).reshape((-1,) + (1,) * (len(dims) - 1 - position))
    return factor_of


def centred(rng, shape, scale, limit, shards=(), held_as=jnp.bfloat16):
    result = jax.random.normal(rng, shape, jnp.float32) * scale
    if len(shards) > 0:
        result = shard_levels(rng, shape, shards, -0.22, 0.18) * result
    return jnp.clip(result, min=-limit, max=limit).astype(held_as)


def setup_inputs(seed: int = 0) -> dict:
    key_of = jax.random.split(jax.random.key(seed), 8)
    iterate = centred(key_of[0], (P_SIZE, NODES), 0.05, 0.75, ((0, 4), (1, 8)), jnp.float32)
    newton_residual = centred(key_of[1], (P_SIZE, NODES), 1.0, 6.0, ((0, 4), (1, 8)), jnp.float32)
    inverse_blocks = draw_inverse_blocks(jax.random.fold_in(key_of[7], 71), 0)
    basis_values = draw_basis_values(jax.random.fold_in(key_of[7], 71), 0)
    triple_blocks = centred(key_of[4], (NB, MB, NNZB * MB * K), (NNZB * MB) ** -0.5, 0.375, ((0, 4), (2, 8)))
    block_columns = draw_block_columns(jax.random.fold_in(key_of[7], 71), 0)
    neighbour_ids = draw_neighbour_ids(jax.random.fold_in(key_of[7], 71), 0)
    return {"iterate": iterate, "newton_residual": newton_residual, "inverse_blocks": inverse_blocks, "basis_values": basis_values, "triple_blocks": triple_blocks, "block_columns": block_columns, "neighbour_ids": neighbour_ids}


GROWTH = 0.5
TIME_STEP = 0.03
LIFT_SCALE = 6.0
PENALTY = 3.0
RELAX_WEIGHT = 0.8
FACE_AXIS = (1, 1, 2, 2, 0, 0)
FACE_SIGN = (-1.0, 1.0, -1.0, 1.0, -1.0, 1.0)
FACE_OPPOSITE = (1, 0, 3, 2, 5, 4)

def line_derivative():
    inward = 1.0 / math.sqrt(5.0)
    points = np.array([-1.0, -inward, inward, 1.0])
    legendre = (5.0 * points ** 3 - 3.0 * points) / 2.0
    matrix = np.zeros((4, 4))
    for source in range(4):
        for target in range(4):
            if source != target:
                matrix[source, target] = legendre[source] / (legendre[target] * (points[source] - points[target]))
    matrix[0, 0] = -3.0
    matrix[3, 3] = 3.0
    return matrix

def direction_tables():
    line_matrix = line_derivative()
    identity = np.eye(4)
    singles = [np.kron(np.kron(line_matrix, identity), identity), np.kron(np.kron(identity, line_matrix), identity), np.kron(np.kron(identity, identity), line_matrix)]
    return [np.kron(np.eye(2), single).T.astype(np.float32) for single in singles]

def face_nodes():
    layout = np.arange(64).reshape(4, 4, 4)
    return np.stack([layout[:, 0, :].ravel(), layout[:, 3, :].ravel(), layout[:, :, 0].ravel(), layout[:, :, 3].ravel(), layout[0].ravel(), layout[3].ravel()])

def embed_table():
    nodes_list = face_nodes()
    table_out = np.zeros((96, 64), np.float32)
    for face_index in range(6):
        for within in range(16):
            table_out[face_index * 16 + within, nodes_list[face_index, within]] = 1.0
    return table_out

def volume_derivative(field, single):
    modes_count = field.shape[0]
    paired = field.reshape(-1, 128)
    return jnp.dot(paired, single, precision=lax.Precision.HIGHEST).reshape(modes_count, -1)

def apply_inverse(field, inverse_blocks):
    modes_count = field.shape[0]
    shaped = field.reshape(modes_count, -1, 64)
    inverse = inverse_blocks.reshape(64, -1, 64)
    return jnp.einsum('mer,req->meq', shaped, inverse, precision=lax.Precision.HIGHEST).reshape(modes_count, -1)

def own_traces(values, flux_fields, face_index, axis_index):
    nodes_list = face_nodes()
    return (values[:, :, nodes_list[face_index]], flux_fields[axis_index][:, :, nodes_list[face_index]])

def lift_terms(values, flux_fields, sources, near_ids, embed_matrix):
    pieces = []
    for face_index in range(6):
        own_values, own_fluxes = own_traces(values, flux_fields, face_index, FACE_AXIS[face_index])
        near_values = jnp.take(sources[face_index][0], near_ids[:, face_index], axis=1)
        near_fluxes = jnp.take(sources[face_index][1], near_ids[:, face_index], axis=1)
        pieces.append(LIFT_SCALE * (0.5 * FACE_SIGN[face_index] * (near_fluxes - own_fluxes) + PENALTY * (near_values - own_values)))
    joined = jnp.concatenate(pieces, axis=2)
    return jnp.einsum('mef,fq->meq', joined, embed_matrix, precision=lax.Precision.HIGHEST)

def neighbour_index(neighbour_ids):
    element_total = neighbour_ids.shape[0]
    owner_block = jnp.arange(element_total, dtype=jnp.int32) // E_DEV
    shifts = jnp.array([0, 0, 0, 0, -1, 1], dtype=jnp.int32)
    blocks = (owner_block[:, None] + shifts[None, :]) % N_ELEM
    return (blocks * E_DEV + neighbour_ids).astype(jnp.int32)

def triple_product(gradients, coeff_terms, triple_blocks, block_columns):
    block_width = triple_blocks.shape[1]
    nodes_count = gradients.shape[2]
    spread = coeff_terms.astype(jnp.float32)
    term_count = spread.shape[0]

    def one_row(operands):
        stored, columns = operands

        def add_block(stored_index, running):
            offset = (columns[stored_index] * block_width).astype(jnp.int32)
            picked = lax.dynamic_slice_in_dim(gradients, offset, block_width, 1)
            expanded = (picked.astype(jnp.float32)[:, :, None, :] * spread[None, None, :, :]).astype(jnp.bfloat16)
            expanded = expanded.reshape(3, block_width * term_count, nodes_count)
            weights = lax.dynamic_slice_in_dim(stored, (stored_index * block_width * term_count).astype(jnp.int32), block_width * term_count, 1)
            return running + jnp.einsum('il,cln->cin', weights.astype(jnp.float32), expanded.astype(jnp.float32))
        return lax.fori_loop(0, columns.shape[0], add_block, jnp.zeros((3, block_width, nodes_count), jnp.float32))
    per_row = lax.map(one_row, (triple_blocks, block_columns))
    return per_row.transpose(1, 0, 2, 3).reshape(3, -1, nodes_count).astype(jnp.bfloat16)

def apply_jacobian(iterate_now, coeff_terms, triple_blocks, block_columns, global_ids, tables, embed_matrix):
    modes_count = iterate_now.shape[0]
    gradients = jnp.stack([volume_derivative(iterate_now, single) for single in tables]).astype(jnp.bfloat16)
    fluxes = triple_product(gradients, coeff_terms, triple_blocks, block_columns)
    values = iterate_now.reshape(modes_count, -1, 64)
    flux_fields = fluxes.astype(jnp.float32).reshape(3, modes_count, -1, 64)
    sources = [own_traces(values, flux_fields, FACE_OPPOSITE[face_index], FACE_AXIS[face_index]) for face_index in range(6)]
    lifted = lift_terms(values, flux_fields, sources, global_ids, embed_matrix)
    divergence = lifted.reshape(modes_count, -1)
    for axis_index in range(3):
        divergence = divergence + volume_derivative(flux_fields[axis_index].reshape(modes_count, -1), tables[axis_index])
    return iterate_now - TIME_STEP * divergence

def reference(iterate, newton_residual, inverse_blocks, basis_values, triple_blocks, block_columns, neighbour_ids):
    tables = [jnp.asarray(single) for single in direction_tables()]
    embed_matrix = jnp.asarray(embed_table())
    global_ids = neighbour_index(neighbour_ids)
    low_state = iterate.astype(jnp.bfloat16)
    sampled = jnp.dot(basis_values, low_state, preferred_element_type=jnp.float32)
    growth = jnp.exp(GROWTH * sampled)
    leading = basis_values[:, :K].astype(jnp.float32)
    coeff_terms = (jnp.dot(leading.T, growth, precision=lax.Precision.HIGHEST) / S).astype(jnp.bfloat16)
    correction = apply_inverse(newton_residual, inverse_blocks)
    remainder = newton_residual
    for sweep_index in range(ITERS):
        applied = apply_jacobian(correction, coeff_terms, triple_blocks, block_columns, global_ids, tables, embed_matrix)
        remainder = newton_residual - applied
        correction = correction + RELAX_WEIGHT * apply_inverse(remainder, inverse_blocks)
    return (correction, remainder)
```

```python
import functools
import math

import jax
import jax.numpy as jnp
import numpy as np
from jax import lax
from jax.experimental import pallas as pl
from jax.experimental.pallas import tpu as pltpu
from jax.sharding import PartitionSpec as P

K = 84
S = 1024
ITERS = 2
MB = 60

GROWTH = 0.5
TIME_STEP = 0.03
LIFT_SCALE = 6.0
PENALTY = 3.0
RELAX_WEIGHT = 0.8
FACE_AXIS = (1, 1, 2, 2, 0, 0)
FACE_SIGN = (-1.0, 1.0, -1.0, 1.0, -1.0, 1.0)
FACE_OPPOSITE = (1, 0, 3, 2, 5, 4)
ROWS = 64
BF = jnp.bfloat16
F32 = jnp.float32
HALF = 512
VMEM = 56 * 2**20


def line_derivative():
    inward = 1.0 / math.sqrt(5.0)
    points = np.array([-1.0, -inward, inward, 1.0])
    legendre = (5.0 * points**3 - 3.0 * points) / 2.0
    matrix = np.zeros((4, 4))
    for source in range(4):
        for target in range(4):
            if source != target:
                matrix[source, target] = legendre[source] / (
                    legendre[target] * (points[source] - points[target])
                )
    matrix[0, 0] = -3.0
    matrix[3, 3] = 3.0
    return matrix


def direction_tables():
    line_matrix = line_derivative()
    identity = np.eye(4)
    singles = [
        np.kron(np.kron(line_matrix, identity), identity),
        np.kron(np.kron(identity, line_matrix), identity),
        np.kron(np.kron(identity, identity), line_matrix),
    ]
    return [np.kron(np.eye(2), single).T for single in singles]


def face_nodes():
    layout = np.arange(64).reshape(4, 4, 4)
    return np.stack(
        [
            layout[:, 0, :].ravel(),
            layout[:, 3, :].ravel(),
            layout[:, :, 0].ravel(),
            layout[:, :, 3].ravel(),
            layout[0].ravel(),
            layout[3].ravel(),
        ]
    )


def high_low(matrix):
    matrix = jnp.asarray(matrix, F32)
    high = matrix.astype(BF)
    return high, (matrix - high.astype(F32)).astype(BF)


def gradient_table():
    return jnp.concatenate(high_low(np.concatenate(direction_tables(), axis=1)), axis=0)


def own_table():
    parts = direction_tables()
    nodes = face_nodes()
    for face in range(6):
        for pair in range(2):
            at = nodes[face] + 64 * pair
            parts[FACE_AXIS[face]][at, at] -= LIFT_SCALE * 0.5 * FACE_SIGN[face]
    return jnp.concatenate(high_low(np.concatenate(parts, axis=0)), axis=0)


def own_weight(lanes):
    counts = np.zeros(64, np.float32)
    for row in face_nodes():
        counts[row] += LIFT_SCALE * PENALTY
    return jnp.asarray(np.tile(counts, lanes // 64)[None, :])


def compaction_tables():
    nodes = face_nodes()
    out = np.zeros((6, HALF, HALF // 4), np.float32)
    for face in range(6):
        for element in range(HALF // 64):
            for within in range(16):
                out[face, element * 64 + nodes[FACE_OPPOSITE[face], within], element * 16 + within] = 1.0
    return jnp.asarray(out, BF)


def lane_ids(neighbour_ids):
    nodes = face_nodes()
    place = np.full((6, 64), -(10**6), np.int32)
    for face in range(6):
        place[face, nodes[face]] = np.arange(16)
    ids = neighbour_ids.T[:, :, None] * 16 + jnp.asarray(place)[:, None, :]
    return ids.reshape(6, -1).astype(jnp.int32)


def precondition(field, inverse, out_ref):
    rows, lanes = field.shape
    row_id = lax.broadcasted_iota(jnp.int32, (128, 128), 0) // 64
    lane_id = lax.broadcasted_iota(jnp.int32, (128, 128), 1) // 64
    same = row_id == lane_id
    for group in range(lanes // 128):
        at = slice(group * 128, group * 128 + 128)
        block = inverse[:, at]
        block = jnp.where(same, jnp.concatenate([block, block], axis=0), 0.0)
        out_ref[:, at] = jnp.dot(
            field[:, at], block, precision=lax.Precision.HIGHEST, preferred_element_type=F32
        )


def centre(field, v_ref):
    row_id = lax.broadcasted_iota(jnp.int32, (128, 128), 0) // 64
    lane_id = lax.broadcasted_iota(jnp.int32, (128, 128), 1) // 64
    average = jnp.where(row_id == lane_id, 1.0 / 64, 0.0).astype(BF)
    for group in range(field.shape[1] // 128):
        at = slice(group * 128, group * 128 + 128)
        part = field[:, at]
        mean = jnp.dot(part.astype(BF), average, preferred_element_type=F32)
        v_ref[:, at] = (part - mean).astype(BF)


def start_kernel(residual_ref, inverse_ref, w_ref, v_ref):
    precondition(residual_ref[...], inverse_ref[...], w_ref)
    centre(w_ref[...], v_ref)


def triple_kernel(chunk, columns_ref, v_ref, c_ref, t_ref, w_ref, grad_ref, pick_ref,
                  flux_ref, trace_ref, g_ref, acc_ref):
    block_rows, depth, _ = t_ref.shape
    nodes = v_ref.shape[2]
    stored = columns_ref.shape[1]
    tile = 512
    for row in range(block_rows):
        for s in range(stored):
            picked = v_ref[columns_ref[row, s]]
            at_rows = slice(s * ROWS, s * ROWS + ROWS)
            for group in range(nodes // 128):
                part = picked[:, group * 128 : group * 128 + 128]
                part = jnp.concatenate([part, part], axis=1)
                grads = jnp.dot(part, grad_ref[...], preferred_element_type=F32).astype(BF)
                for d in range(3):
                    first = d * nodes + group * 128
                    g_ref[at_rows, first : first + 128] = grads[:, d * 128 : d * 128 + 128]
        acc_ref[...] = jnp.zeros_like(acc_ref)

        def one_chunk(index, carry):
            width = chunk * ROWS
            weights = t_ref[row, :, pl.ds(pl.multiple_of(index * width, 128), width)].T
            for first in range(0, 3 * nodes, tile):
                at = slice(first, first + tile)
                product = jnp.dot(weights, g_ref[:, at], preferred_element_type=F32)
                total = acc_ref[:, at]
                node = first % nodes
                for k in range(chunk):
                    coefficient = c_ref[pl.ds(index * chunk + k, 1), node : node + tile]
                    total = total + product[k * ROWS : k * ROWS + ROWS] * coefficient
                acc_ref[:, at] = total
            return carry

        lax.fori_loop(0, K // chunk, one_chunk, 0)
        for d in range(3):
            flux_ref[d, row * ROWS : row * ROWS + ROWS, :] = acc_ref[
                :, d * nodes : d * nodes + nodes
            ].astype(BF)
    count = w_ref.shape[0]
    for face in range(6):
        mixed = LIFT_SCALE * PENALTY * w_ref[...] + (
            LIFT_SCALE * 0.5 * FACE_SIGN[face]
        ) * flux_ref[FACE_AXIS[face]].astype(F32)
        high = mixed.astype(BF)
        low = (mixed - high.astype(F32)).astype(BF)
        for half in range(nodes // HALF):
            at = slice(half * HALF, half * HALF + HALF)
            to = slice(half * HALF // 4, half * HALF // 4 + HALF // 4)
            trace_ref[face, :count, to] = jnp.dot(
                high[:, at], pick_ref[face], preferred_element_type=F32
            ).astype(BF)
            trace_ref[face, count:, to] = jnp.dot(
                low[:, at], pick_ref[face], preferred_element_type=F32
            ).astype(BF)


def finish_kernel(w_ref, residual_ref, inverse_ref, flux_ref, near_ref, before_ref, after_ref,
                  ids_ref, own_ref, weight_ref, corr_ref, lin_ref, v_ref):
    count, nodes = w_ref.shape
    for group in range(nodes // 128):
        at = slice(group * 128, group * 128 + 128)
        parts = [flux_ref[d, :, at] for d in range(3)]
        parts = jnp.concatenate(parts + parts, axis=1)
        lin_ref[:, at] = jnp.dot(parts, own_ref[...], preferred_element_type=F32)
    tile = 256
    for first in range(0, nodes, tile):
        at = slice(first, first + tile)
        total = lin_ref[:, at] - weight_ref[:, at] * w_ref[:, at]
        for face in range(6):
            if face < 4:
                trace = near_ref[face]
            else:
                trace = (before_ref if face == 4 else after_ref)[...]
            rows = lax.broadcasted_iota(jnp.int32, (trace.shape[1], tile), 0)
            spread = jnp.where(rows == ids_ref[face : face + 1, at], 1.0, 0.0).astype(BF)
            got = jnp.dot(trace, spread, preferred_element_type=F32)
            total = total + got[:count] + got[count:]
        lin_ref[:, at] = residual_ref[:, at] - (w_ref[:, at] - TIME_STEP * total)
    precondition(lin_ref[...], inverse_ref[...], corr_ref)
    corr_ref[...] = w_ref[...] + RELAX_WEIGHT * corr_ref[...]
    centre(corr_ref[...], v_ref)


VM = pl.BlockSpec(memory_space=pltpu.VMEM)
SM = pl.BlockSpec(memory_space=pltpu.SMEM)


def call(kernel, outs, ins, scratch=(), name=None):
    return pl.pallas_call(
        kernel,
        out_shape=outs,
        in_specs=ins,
        out_specs=[VM] * len(outs),
        scratch_shapes=list(scratch),
        compiler_params=pltpu.CompilerParams(vmem_limit_bytes=VMEM),
        name=name,
    )


def per_device(
    iterate,
    newton_residual,
    inverse_blocks,
    basis_values,
    triple_blocks,
    block_columns,
    neighbour_ids,
):
    modes, nodes = iterate.shape
    block_rows = triple_blocks.shape[0]
    shard = triple_blocks.shape[2] // K
    elem_count = lax.axis_size("elem")
    groups = MB // shard
    wide = ROWS // groups

    def pad_modes(field):
        field = field.reshape(modes // shard, shard, nodes)
        return jnp.pad(field, ((0, 0), (0, wide - shard), (0, 0))).reshape(-1, nodes)

    def unpad_modes(field):
        return field.reshape(modes // shard, wide, nodes)[:, :shard].reshape(modes, nodes)

    blocks = triple_blocks.reshape(block_rows, groups, shard, shard, K)
    blocks = blocks.transpose(0, 3, 4, 1, 2)
    blocks = jnp.pad(blocks, ((0, 0), (0, wide - shard), (0, 0), (0, 0), (0, wide - shard)))
    blocks = blocks.reshape(block_rows, wide, K * ROWS)
    blocks = lax.all_gather(blocks, "elem", axis=1, tiled=True)

    low_state = iterate.astype(BF)
    regrouped = lax.all_to_all(low_state, "mode", split_axis=1, concat_axis=0, tiled=True)
    sampled = jnp.dot(basis_values, regrouped, preferred_element_type=F32)
    growth = jnp.exp(GROWTH * sampled)
    leading = basis_values[:, :K]
    high = growth.astype(BF)
    low = (growth - high.astype(F32)).astype(BF)
    contract = functools.partial(
        lax.dot_general, dimension_numbers=(((0,), (0,)), ((), ())), preferred_element_type=F32
    )
    node_terms = (contract(leading, high) + contract(leading, low)) / S
    coeff_terms = lax.all_gather(node_terms.astype(BF), "mode", axis=1, tiled=True).astype(F32)

    residual = pad_modes(newton_residual)
    rows = residual.shape[0]
    field = jax.ShapeDtypeStruct((rows, nodes), F32)
    low_field = jax.ShapeDtypeStruct((rows, nodes), BF)
    ids = lane_ids(neighbour_ids)
    w, v = call(start_kernel, [field, low_field], [VM] * 2, name="start")(residual, inverse_blocks)
    forward = [(i, (i + 1) % elem_count) for i in range(elem_count)]
    backward = [(target, source) for source, target in forward]
    grads, picks, owns, weight = gradient_table(), compaction_tables(), own_table(), own_weight(nodes)
    lin = None
    for sweep in range(ITERS):
        gathered = lax.all_gather(v, "mode", axis=0, tiled=True).reshape(-1, ROWS, nodes)
        flux, traces = call(
            functools.partial(triple_kernel, 12),
            [
                jax.ShapeDtypeStruct((3, rows, nodes), BF),
                jax.ShapeDtypeStruct((6, 2 * rows, nodes // 4), BF),
            ],
            [SM] + [VM] * 6,
            [pltpu.VMEM((blocks.shape[1], 3 * nodes), BF), pltpu.VMEM((ROWS, 3 * nodes), F32)],
            name="triple",
        )(block_columns, gathered, coeff_terms, blocks, w, grads, picks)
        before = lax.ppermute(traces[4], "elem", forward)
        after = lax.ppermute(traces[5], "elem", backward)
        w, lin, v = call(finish_kernel, [field, field, low_field], [VM] * 10, name="finish")(
            w, residual, inverse_blocks, flux, traces, before, after, ids, owns, weight
        )
    return (unpad_modes(w), unpad_modes(lin))


def solution(mesh):
    return jax.shard_map(
        per_device,
        mesh=mesh,
        in_specs=(
            P("mode", "elem"),
            P("mode", "elem"),
            P(None, "elem"),
            P(),
            P("mode", None, "elem"),
            P("mode", None),
            P("elem", None),
        ),
        out_specs=(P("mode", "elem"), P("mode", "elem")),
        check_vma=False,
    )
```

```python
import functools
import math

import jax
import jax.numpy as jnp
import numpy as np
from jax import lax
from jax.experimental import pallas as pl
from jax.experimental.pallas import tpu as pltpu
from jax.sharding import PartitionSpec as P

K = 84
S = 1024
ITERS = 2
MB = 60

GROWTH = 0.5
TIME_STEP = 0.03
LIFT_SCALE = 6.0
PENALTY = 3.0
RELAX_WEIGHT = 0.8
FACE_AXIS = (1, 1, 2, 2, 0, 0)
FACE_SIGN = (-1.0, 1.0, -1.0, 1.0, -1.0, 1.0)
FACE_OPPOSITE = (1, 0, 3, 2, 5, 4)
ROWS = 64
BF = jnp.bfloat16
F32 = jnp.float32
HALF = 512
VMEM = 56 * 2**20


def line_derivative():
    inward = 1.0 / math.sqrt(5.0)
    points = np.array([-1.0, -inward, inward, 1.0])
    legendre = (5.0 * points**3 - 3.0 * points) / 2.0
    matrix = np.zeros((4, 4))
    for source in range(4):
        for target in range(4):
            if source != target:
                matrix[source, target] = legendre[source] / (
                    legendre[target] * (points[source] - points[target])
                )
    matrix[0, 0] = -3.0
    matrix[3, 3] = 3.0
    return matrix


def direction_tables():
    line_matrix = line_derivative()
    identity = np.eye(4)
    singles = [
        np.kron(np.kron(line_matrix, identity), identity),
        np.kron(np.kron(identity, line_matrix), identity),
        np.kron(np.kron(identity, identity), line_matrix),
    ]
    return [np.kron(np.eye(2), single).T for single in singles]


def face_nodes():
    layout = np.arange(64).reshape(4, 4, 4)
    return np.stack(
        [
            layout[:, 0, :].ravel(),
            layout[:, 3, :].ravel(),
            layout[:, :, 0].ravel(),
            layout[:, :, 3].ravel(),
            layout[0].ravel(),
            layout[3].ravel(),
        ]
    )


def high_low(matrix):
    matrix = jnp.asarray(matrix, F32)
    high = matrix.astype(BF)
    return high, (matrix - high.astype(F32)).astype(BF)


def gradient_table():
    return jnp.concatenate(high_low(np.concatenate(direction_tables(), axis=1)), axis=0)


def own_table():
    parts = direction_tables()
    nodes = face_nodes()
    for face in range(6):
        for pair in range(2):
            at = nodes[face] + 64 * pair
            parts[FACE_AXIS[face]][at, at] -= LIFT_SCALE * 0.5 * FACE_SIGN[face]
    return jnp.concatenate(high_low(np.concatenate(parts, axis=0)), axis=0)


def own_weight(lanes):
    counts = np.zeros(64, np.float32)
    for row in face_nodes():
        counts[row] += LIFT_SCALE * PENALTY
    return jnp.asarray(np.tile(counts, lanes // 64)[None, :])


def compaction_tables():
    nodes = face_nodes()
    out = np.zeros((6, HALF, HALF // 4), np.float32)
    for face in range(6):
        for element in range(HALF // 64):
            for within in range(16):
                out[face, element * 64 + nodes[FACE_OPPOSITE[face], within], element * 16 + within] = 1.0
    return jnp.asarray(out, BF)


def lane_ids(neighbour_ids):
    nodes = face_nodes()
    place = np.full((6, 64), -(10**6), np.int32)
    for face in range(6):
        place[face, nodes[face]] = np.arange(16)
    ids = neighbour_ids.T[:, :, None] * 16 + jnp.asarray(place)[:, None, :]
    return ids.reshape(6, -1).astype(jnp.int32)


def precondition(field, inverse, out_ref):
    rows, lanes = field.shape
    row_id = lax.broadcasted_iota(jnp.int32, (128, 128), 0) // 64
    lane_id = lax.broadcasted_iota(jnp.int32, (128, 128), 1) // 64
    same = row_id == lane_id
    for group in range(lanes // 128):
        at = slice(group * 128, group * 128 + 128)
        block = inverse[:, at]
        block = jnp.where(same, jnp.concatenate([block, block], axis=0), 0.0)
        out_ref[:, at] = jnp.dot(
            field[:, at], block, precision=lax.Precision.HIGHEST, preferred_element_type=F32
        )


def centre(field, v_ref):
    row_id = lax.broadcasted_iota(jnp.int32, (128, 128), 0) // 64
    lane_id = lax.broadcasted_iota(jnp.int32, (128, 128), 1) // 64
    average = jnp.where(row_id == lane_id, 1.0 / 64, 0.0).astype(BF)
    for group in range(field.shape[1] // 128):
        at = slice(group * 128, group * 128 + 128)
        part = field[:, at]
        mean = jnp.dot(part.astype(BF), average, preferred_element_type=F32)
        v_ref[:, at] = (part - mean).astype(BF)


MESH = pl.DeviceIdType.MESH


def greet(devices):
    barrier = pltpu.get_barrier_semaphore()
    for device in devices:
        pl.semaphore_signal(barrier, inc=1, device_id=device, device_id_type=MESH)
    pl.semaphore_wait(barrier, len(devices))


def push(source, target, send, receive, device):
    copy = pltpu.make_async_remote_copy(
        src_ref=source,
        dst_ref=target,
        send_sem=send,
        recv_sem=receive,
        device_id=device,
        device_id_type=MESH,
    )
    copy.start()
    return copy


def start_kernel(mode_count, elem_count, t_ref, low_ref, basis_ref, leading_ref, residual_ref,
                 inverse_ref, t_all, v_all, c_all, w_ref, low_all, growth_ref,
                 own_sem, t_sem, mate_sem, low_sem, v_sem, c_sem):
    m, e = lax.axis_index("mode"), lax.axis_index("elem")
    pairs = elem_count // 2
    mate = (e + 1 - 2 * lax.rem(e, 2), m)
    across = [None] + [(lax.rem(e + 2 * k, elem_count), m) for k in range(1, pairs)]
    along = [None] + [(e, lax.rem(m + k, mode_count)) for k in range(1, mode_count)]
    greet([mate] + across[1:] + along[1:])
    copies = []
    for k in range(1, mode_count):
        copies.append(
            push(low_ref.at[along[k][1]], low_all.at[m], low_sem.at[0, k], low_sem.at[1, k], along[k])
        )
    lows = list(copies)
    blocks = [
        push(t_ref, t_all.at[e], t_sem.at[0, k], t_sem.at[1, k], across[k]) for k in range(1, pairs)
    ]
    mates = [push(t_ref, t_all.at[e], mate_sem.at[0, 0], mate_sem.at[1, 0], mate)]
    own = pltpu.make_async_copy(t_ref, t_all.at[e], own_sem)
    own.start()
    low_all[m] = low_ref[m]
    precondition(residual_ref[...], inverse_ref[...], w_ref)
    centre(w_ref[...], v_all.at[m])
    fields = [
        push(v_all.at[m], v_all.at[m], v_sem.at[0, k], v_sem.at[1, k], along[k])
        for k in range(1, mode_count)
    ]
    for copy in lows:
        copy.wait_recv()
    state = low_all[...].reshape(-1, low_all.shape[2])
    sampled = jnp.dot(basis_ref[...], state, preferred_element_type=F32)
    growth_ref[...] = jnp.exp(GROWTH * sampled)
    high = growth_ref[...].astype(BF)
    low = (growth_ref[...] - high.astype(F32)).astype(BF)
    terms = jnp.dot(leading_ref[...], high, preferred_element_type=F32)
    terms = terms + jnp.dot(leading_ref[...], low, preferred_element_type=F32)
    c_all[m] = (terms / S).astype(BF)
    terms_out = [
        push(c_all.at[m], c_all.at[m], c_sem.at[0, k], c_sem.at[1, k], along[k])
        for k in range(1, mode_count)
    ]
    for k in range(1, pairs):
        blocks[k - 1].wait_recv()
        got = lax.rem(e + elem_count - 2 * k, elem_count)
        mates.append(push(t_all.at[got], t_all.at[got], mate_sem.at[0, k], mate_sem.at[1, k], mate))
    for copy in lows + blocks:
        copy.wait_send()
    for copy in fields + terms_out + mates:
        copy.wait()
    own.wait()


def triple_kernel(chunk, columns_ref, v_ref, c_ref, t_ref, w_ref, grad_ref, pick_ref,
                  flux_ref, trace_ref, g_ref, acc_ref):
    shards, block_rows, wide, _ = t_ref.shape
    depth = shards * wide
    nodes = v_ref.shape[2]
    stored = columns_ref.shape[1]
    tile = 512
    for row in range(block_rows):
        for s in range(stored):
            picked = v_ref[columns_ref[row, s]]
            at_rows = slice(s * ROWS, s * ROWS + ROWS)
            for group in range(nodes // 128):
                part = picked[:, group * 128 : group * 128 + 128]
                part = jnp.concatenate([part, part], axis=1)
                grads = jnp.dot(part, grad_ref[...], preferred_element_type=F32).astype(BF)
                for d in range(3):
                    first = d * nodes + group * 128
                    g_ref[at_rows, first : first + 128] = grads[:, d * 128 : d * 128 + 128]
        acc_ref[...] = jnp.zeros_like(acc_ref)

        def one_chunk(index, carry):
            width = chunk * ROWS
            weights = t_ref[:, row, :, pl.ds(pl.multiple_of(index * width, 128), width)]
            weights = weights.reshape(depth, width).T
            for first in range(0, 3 * nodes, tile):
                at = slice(first, first + tile)
                product = jnp.dot(weights, g_ref[:, at], preferred_element_type=F32)
                total = acc_ref[:, at]
                node = first % nodes
                for k in range(chunk):
                    coefficient = c_ref[pl.ds(index * chunk + k, 1), node : node + tile]
                    total = total + product[k * ROWS : k * ROWS + ROWS] * coefficient
                acc_ref[:, at] = total
            return carry

        lax.fori_loop(0, K // chunk, one_chunk, 0)
        for d in range(3):
            flux_ref[d, row * ROWS : row * ROWS + ROWS, :] = acc_ref[
                :, d * nodes : d * nodes + nodes
            ].astype(BF)
    count = w_ref.shape[0]
    for face in range(6):
        mixed = LIFT_SCALE * PENALTY * w_ref[...] + (
            LIFT_SCALE * 0.5 * FACE_SIGN[face]
        ) * flux_ref[FACE_AXIS[face]].astype(F32)
        high = mixed.astype(BF)
        low = (mixed - high.astype(F32)).astype(BF)
        for half in range(nodes // HALF):
            at = slice(half * HALF, half * HALF + HALF)
            to = slice(half * HALF // 4, half * HALF // 4 + HALF // 4)
            trace_ref[face, :count, to] = jnp.dot(
                high[:, at], pick_ref[face], preferred_element_type=F32
            ).astype(BF)
            trace_ref[face, count:, to] = jnp.dot(
                low[:, at], pick_ref[face], preferred_element_type=F32
            ).astype(BF)


def finish_kernel(mode_count, elem_count, last, w_ref, residual_ref, inverse_ref, flux_ref, near_ref,
                  ids_ref, own_ref, weight_ref, *refs):
    if last:
        corr_ref, lin_ref, side_ref, side_sem = refs
        v_all, v_sem = None, None
    else:
        corr_ref, lin_ref, v_all, side_ref, side_sem, v_sem = refs
    count, nodes = w_ref.shape
    m, e = lax.axis_index("mode"), lax.axis_index("elem")
    after = (lax.rem(e + 1, elem_count), m)
    before = (lax.rem(e + elem_count - 1, elem_count), m)
    along = [(e, lax.rem(m + k, mode_count)) for k in range(1, mode_count)]
    greet([before, after] + ([] if last else along))
    sides = [
        push(near_ref.at[4], side_ref.at[0], side_sem.at[0, 0], side_sem.at[1, 0], after),
        push(near_ref.at[5], side_ref.at[1], side_sem.at[0, 1], side_sem.at[1, 1], before),
    ]
    for group in range(nodes // 128):
        at = slice(group * 128, group * 128 + 128)
        parts = [flux_ref[d, :, at] for d in range(3)]
        parts = jnp.concatenate(parts + parts, axis=1)
        lin_ref[:, at] = jnp.dot(parts, own_ref[...], preferred_element_type=F32)
    tile = 256

    def spread_faces(total, traces, faces, at):
        for trace, face in zip(traces, faces):
            rows = lax.broadcasted_iota(jnp.int32, (trace.shape[1], tile), 0)
            spread = jnp.where(rows == ids_ref[face : face + 1, at], 1.0, 0.0).astype(BF)
            got = jnp.dot(trace, spread, preferred_element_type=F32)
            total = total + got[:count] + got[count:]
        return total

    for first in range(0, nodes, tile):
        at = slice(first, first + tile)
        total = lin_ref[:, at] - weight_ref[:, at] * w_ref[:, at]
        lin_ref[:, at] = spread_faces(total, [near_ref[f] for f in range(4)], range(4), at)
    for copy in sides:
        copy.wait()
    sent = []
    for index, first in enumerate(range(0, nodes, tile)):
        at = slice(first, first + tile)
        total = spread_faces(lin_ref[:, at], [side_ref[0], side_ref[1]], (4, 5), at)
        lin_ref[:, at] = residual_ref[:, at] - (w_ref[:, at] - TIME_STEP * total)
        precondition(lin_ref[:, at], inverse_ref[:, at], corr_ref.at[:, pl.ds(first, tile)])
        corr_ref[:, at] = w_ref[:, at] + RELAX_WEIGHT * corr_ref[:, at]
        if not last:
            part = v_all.at[m, :, pl.ds(first, tile)]
            centre(corr_ref[:, at], part)
            for k in range(1, mode_count):
                sent.append(
                    push(part, part, v_sem.at[0, index, k], v_sem.at[1, index, k], along[k - 1])
                )
    for copy in sent:
        copy.wait()


VM = pl.BlockSpec(memory_space=pltpu.VMEM)
SM = pl.BlockSpec(memory_space=pltpu.SMEM)


AN = pl.BlockSpec(memory_space=pl.ANY)


def call(kernel, outs, ins, scratch=(), name=None, out_specs=None, remote=None):
    more = {} if remote is None else {"collective_id": remote, "has_side_effects": True}
    return pl.pallas_call(
        kernel,
        out_shape=outs,
        in_specs=ins,
        out_specs=out_specs or [VM] * len(outs),
        scratch_shapes=list(scratch),
        compiler_params=pltpu.CompilerParams(vmem_limit_bytes=VMEM, **more),
        name=name,
    )


def per_device(
    iterate,
    newton_residual,
    inverse_blocks,
    basis_values,
    triple_blocks,
    block_columns,
    neighbour_ids,
):
    modes, nodes = iterate.shape
    block_rows = triple_blocks.shape[0]
    shard = triple_blocks.shape[2] // K
    elem_count = lax.axis_size("elem")
    groups = MB // shard
    wide = ROWS // groups

    def pad_modes(field):
        field = field.reshape(modes // shard, shard, nodes)
        return jnp.pad(field, ((0, 0), (0, wide - shard), (0, 0))).reshape(-1, nodes)

    def unpad_modes(field):
        return field.reshape(modes // shard, wide, nodes)[:, :shard].reshape(modes, nodes)

    blocks = triple_blocks.reshape(block_rows, groups, shard, shard, K)
    blocks = blocks.transpose(0, 3, 4, 1, 2)
    blocks = jnp.pad(blocks, ((0, 0), (0, wide - shard), (0, 0), (0, 0), (0, wide - shard)))
    blocks = blocks.reshape(block_rows, wide, K * ROWS)

    mode_count = lax.axis_size("mode")
    share = nodes // mode_count
    low_state = pad_modes(iterate.astype(BF))
    rows = low_state.shape[0]
    low_state = low_state.reshape(rows, mode_count, share).transpose(1, 0, 2)
    basis = jnp.pad(
        basis_values.reshape(S, -1, shard), ((0, 0), (0, 0), (0, wide - shard))
    ).reshape(S, -1)
    terms_rows = -(-K // 16) * 16
    leading = jnp.pad(basis_values[:, :K].T, ((0, terms_rows - K), (0, 0)))

    residual = pad_modes(newton_residual)
    field = jax.ShapeDtypeStruct((rows, nodes), F32)
    all_fields = jax.ShapeDtypeStruct((mode_count, rows, nodes), BF)
    ids = lane_ids(neighbour_ids)
    grads, picks, owns, weight = gradient_table(), compaction_tables(), own_table(), own_weight(nodes)
    dma = pltpu.SemaphoreType.DMA
    blocks, v, terms, w = call(
        functools.partial(start_kernel, mode_count, elem_count),
        [
            jax.ShapeDtypeStruct((elem_count,) + blocks.shape, BF),
            all_fields,
            jax.ShapeDtypeStruct((mode_count, terms_rows, share), BF),
            field,
        ],
        [AN] + [VM] * 5,
        [
            pltpu.VMEM((mode_count, rows, share), BF),
            pltpu.VMEM((S, share), F32),
            dma,
            dma((2, elem_count // 2)),
            dma((2, elem_count // 2)),
            dma((2, mode_count)),
            dma((2, mode_count)),
            dma((2, mode_count)),
        ],
        name="start",
        out_specs=[AN, VM, VM, VM],
        remote=0,
    )(blocks, low_state, basis, leading, residual, inverse_blocks)
    coeff_terms = terms.transpose(1, 0, 2).reshape(terms_rows, nodes).astype(F32)
    lin = None
    for sweep in range(ITERS):
        last = sweep == ITERS - 1
        flux, traces = call(
            functools.partial(triple_kernel, 12),
            [
                jax.ShapeDtypeStruct((3, rows, nodes), BF),
                jax.ShapeDtypeStruct((6, 2 * rows, nodes // 4), BF),
            ],
            [SM] + [VM] * 6,
            [pltpu.VMEM((elem_count * wide, 3 * nodes), BF), pltpu.VMEM((ROWS, 3 * nodes), F32)],
            name="triple",
        )(block_columns, v.reshape(-1, ROWS, nodes), coeff_terms, blocks, w, grads, picks)
        results = call(
            functools.partial(finish_kernel, mode_count, elem_count, last),
            [field, field] + ([] if last else [all_fields]),
            [VM] * 8,
            [pltpu.VMEM((2, 2 * rows, nodes // 4), BF), dma((2, 2))]
            + ([] if last else [dma((2, nodes // 256, mode_count))]),
            name="finish",
            remote=2 if last else 1,
        )(w, residual, inverse_blocks, flux, traces, ids, owns, weight)
        w, lin = results[:2]
        v = None if last else results[2]
    return (unpad_modes(w), unpad_modes(lin))


def solution(mesh):
    return jax.shard_map(
        per_device,
        mesh=mesh,
        in_specs=(
            P("mode", "elem"),
            P("mode", "elem"),
            P(None, "elem"),
            P(),
            P("mode", None, "elem"),
            P("mode", None),
            P("elem", None),
        ),
        out_specs=(P("mode", "elem"), P("mode", "elem")),
        check_vma=False,
    )
```
